32 devices in a mesh: grp: 2 (over y), reg: 4 (over x, core), dev: 4 (over z).
Axes of the slice: x: 2, y: 2, z: 4, core: 2. Of those that a mesh axis runs over, the one named last changes fastest.
Arguments:
- footprints: bfloat16 [4096, 128, 128], P(('grp', 'reg', 'dev')), parts along dimension 0, may hold values from 0.0009994507 to 0.029907227
- block_coords: int32 [4096, 2], P(('grp', 'reg', 'dev')), parts along dimension 0, may hold values from 0 to 127, as said below
- receptor_place: int32 [256], P('grp'), parts along dimension 0, may hold values from 0 to 127, as said below
- source_place: int32 [128], P('grp'), parts along dimension 0, may hold values from 0 to 63, as said below
- probe_matrix: bfloat16 [16384, 256], P(('grp', 'reg', 'dev')), parts along dimension 0, may hold values from -6 to 6
Outputs:
- receptor_image: bfloat16 [32768, 256], P(('grp', 'dev')), parts along dimension 0
- source_image: float32 [16384, 256], P(('grp', 'reg', 'dev')), parts along dimension 0
The draws below stay inside these ranges and needn't reach their ends.
There are 2 independent parts, one for each index of `grp`. The reference program is written for one: setup_inputs(seed, part) draws one part's arguments, and reference() takes and returns one part's arrays. A program takes and returns all parts, laid end to end along the dimension named above; each array names one. Nothing has to cross between parts.
Inputs may be any that keep to these rules, and one draw needn't show every extreme that they name: `block_coords`: the destination of a block is the device whose reg index is pos_src // 16 and whose dev index is pos_rec // 32. The 128 blocks of one device send at most 16 blocks to any one destination, and one particular destination receives exactly 16 from every device (the others may receive fewer). Column 0 is below 128, column 1 below 64. `receptor_place`: A permutation of the receptor blocks. `source_place`: A permutation of the source blocks.
All inputs are finite; a program needn't handle non-finite values.
Results may differ from the reference program's by a relative error of at most 0.0085.
Values may be sent and summed in bfloat16 or wider, within the bound.
A program may use at most 128 MiB of HBM per device.

```python
import math
import jax
import jax.numpy as jnp
from jax import lax

CELLS = 128
PROBES = 256
BLK_DEV = 128
RB_GRP = 32
SB_DEV = 4
OWNERS = 16
CAP = 16
REGION = 16
NRB = 128
NSB = 64
NBLK = 2048


def layout(base_key):
    receptor_order = jax.random.permutation(jax.random.fold_in(base_key, 101), NRB).astype(jnp.int32)
    source_order = jax.random.permutation(jax.random.fold_in(base_key, 102), NSB).astype(jnp.int32)
    return (receptor_order, source_order)


def draw_receptor_place(key, part):
    return layout(key)[0]


def draw_source_place(key, part):
    return layout(key)[1]


def draw_block_coords(key, part):
    receptor_order, source_order = layout(key)
    full_target = jax.random.randint(jax.random.fold_in(key, 103), (), 0, OWNERS).astype(jnp.int32)
    slot_keys = jax.random.split(jax.random.fold_in(key, 104), OWNERS)

    def choose_slots(sub_key):
        chosen = jax.random.permutation(sub_key, (OWNERS - 1) * CAP)[:BLK_DEV - CAP]
        return (chosen // CAP).astype(jnp.int32)
    raw_slot = jax.vmap(choose_slots)(slot_keys)
    others = raw_slot + (raw_slot >= full_target).astype(jnp.int32)
    forced = jnp.zeros((OWNERS, CAP), jnp.int32) + full_target
    targets = jnp.concatenate([forced, others], axis=1)
    shuffle_keys = jax.random.split(jax.random.fold_in(key, 105), OWNERS)
    shuffle = jax.vmap(lambda sub_key: jax.random.permutation(sub_key, BLK_DEV))(shuffle_keys).astype(jnp.int32)
    targets = jnp.take_along_axis(targets, shuffle, axis=1)
    rec_local = jax.random.randint(jax.random.fold_in(key, 106), (OWNERS, BLK_DEV), 0, RB_GRP).astype(jnp.int32)
    src_local = jax.random.randint(jax.random.fold_in(key, 107), (OWNERS, BLK_DEV), 0, REGION).astype(jnp.int32)
    dev_width = REGION // SB_DEV
    pos_rec = targets % dev_width * RB_GRP + rec_local
    pos_src = targets // dev_width * REGION + src_local
    inverse_rec = jnp.zeros((NRB,), jnp.int32).at[receptor_order].set(jnp.arange(NRB, dtype=jnp.int32))
    inverse_src = jnp.zeros((NSB,), jnp.int32).at[source_order].set(jnp.arange(NSB, dtype=jnp.int32))
    coords = jnp.stack([inverse_rec[pos_rec], inverse_src[pos_src]], axis=-1)
    return coords.reshape(NBLK, 2).astype(jnp.int32)


def block_scale(stream_key, shape, cuts, least, high):
    level = 1.0
    for position, parts in cuts:
        steps = jax.random.uniform(jax.random.fold_in(jax.random.fold_in(stream_key, 6), position), (parts,), jnp.float32, least / len(cuts), high / len(cuts))
        level = level * jnp.repeat(jnp.exp(steps), shape[position] // parts).reshape((-1,) + (1,) * (len(shape) - 1 - position))
    return level


def noise(rng, dims, deviation, bound, cuts=(), kind=jnp.bfloat16):
    drawn = deviation * jax.random.normal(rng, dims, jnp.float32)
    if cuts:
        drawn = drawn * block_scale(rng, dims, cuts, -0.22, 0.18)
    return jnp.clip(drawn, -bound, bound).astype(kind)


def setup_inputs(seed: int = 0, part: int = 0) -> dict:
    key_of = jax.random.split(jax.random.key(seed), 6)
    own_keys = jax.random.split(jax.random.fold_in(key_of[5], part), 6)
    return {
        "footprints": jnp.clip(jnp.exp(math.log(0.029907227) - 3.3986496 * jax.random.uniform(own_keys[0], (NBLK, CELLS, CELLS), jnp.float32) ** block_scale(own_keys[0], (NBLK, CELLS, CELLS), ((0, 16),), -0.2, 0.2)), 0.0009994507, 0.029907227).astype(jnp.bfloat16),
        "block_coords": draw_block_coords(jax.random.fold_in(jax.random.fold_in(key_of[5], part), 71), part),
        "receptor_place": draw_receptor_place(jax.random.fold_in(jax.random.fold_in(key_of[5], part), 71), part),
        "source_place": draw_source_place(jax.random.fold_in(jax.random.fold_in(key_of[5], part), 71), part),
        "probe_matrix": noise(own_keys[4], (NSB * CELLS, PROBES), 1.0, 6.0, ((0, 16),)),
    }


def reference(footprints, block_coords, receptor_place, source_place, probe_matrix):
    pos_rec = receptor_place[block_coords[:, 0]].astype(jnp.int32)
    pos_src = source_place[block_coords[:, 1]].astype(jnp.int32)
    group_size = math.gcd(NBLK, 256)
    groups = NBLK // group_size
    grouped_blocks = footprints.reshape(groups, group_size, CELLS, CELLS)
    grouped_rec = pos_rec.reshape(groups, group_size)
    grouped_src = pos_src.reshape(groups, group_size)
    probe_blocks = probe_matrix.reshape(NSB, CELLS, PROBES).astype(jnp.float32)

    def forward_step(running, items):
        pieces, rec_slot, src_slot = items
        taken = probe_blocks[src_slot]
        terms = jnp.einsum("gij,gjk->gik", pieces.astype(jnp.float32), taken)
        return running.at[rec_slot].add(terms), None

    start_rec = jnp.zeros((NRB, CELLS, PROBES), jnp.float32)
    receptor_sum, unused = lax.scan(forward_step, start_rec, (grouped_blocks, grouped_rec, grouped_src))
    receptor_image = receptor_sum.astype(jnp.bfloat16)
    image_wide = receptor_image.astype(jnp.float32)

    def backward_step(running, items):
        pieces, rec_slot, src_slot = items
        taken = image_wide[rec_slot]
        terms = jnp.einsum("gji,gjk->gik", pieces.astype(jnp.float32), taken)
        return running.at[src_slot].add(terms), None

    start_src = jnp.zeros((NSB, CELLS, PROBES), jnp.float32)
    source_sum, unused_two = lax.scan(backward_step, start_src, (grouped_blocks, grouped_rec, grouped_src))
    return receptor_image.reshape(NRB * CELLS, PROBES), source_sum.reshape(NSB * CELLS, PROBES)
```

```python
import functools

import jax
import jax.numpy as jnp
from jax import lax
from jax.experimental import pallas as pl
from jax.experimental.pallas import tpu as pltpu
from jax.sharding import PartitionSpec as P

MESH = pl.DeviceIdType.MESH
ANY = pl.BlockSpec(memory_space=pl.ANY)
VMEM_LIMIT = 60 * 2**20
SPLIT = 2


class Ring:
    def __init__(self, reg, dev):
        self.reg, self.dev = reg, dev
        self.chips = reg // 2 * dev
        self.half = self.chips // 2
        r, z = lax.axis_index("reg"), lax.axis_index("dev")
        x, self.core = r // 2, r % 2
        self.at = x * dev + z + (x % 2) * (dev - 1 - 2 * z)
        self.sign = 1 - 2 * self.core

    def place(self, steps):
        at = lax.rem(self.at + steps + 2 * self.chips, self.chips)
        x, z = at // self.dev, at % self.dev
        return x, z + (x % 2) * (self.dev - 1 - 2 * z)

    def device(self, steps, other=0):
        x, z = self.place(steps)
        return {"reg": 2 * x + (self.core if not other else 1 - self.core), "dev": z}

    def chunk(self, by_dev, steps, other=0):
        x, z = self.place(steps)
        r = 2 * x + (self.core if not other else 1 - self.core)
        return z * self.reg + r if by_dev else r * self.dev + z

    def partners(self):
        return self.device(self.sign), self.device(-self.sign), self.device(0, 1)

    def barrier(self):
        barrier = pltpu.get_barrier_semaphore()
        for who in self.partners():
            pl.semaphore_signal(barrier, inc=1, device_id=who, device_id_type=MESH)
        pl.semaphore_wait(barrier, 3)


def remote(src, dst, send, recv, who):
    return pltpu.make_async_remote_copy(
        src_ref=src, dst_ref=dst, send_sem=send, recv_sem=recv, device_id=who, device_id_type=MESH
    )


def order_of_use(half):
    order = []
    for step in range(half):
        order.append(("a", step))
        if step < half - 1:
            order.append(("b", step))
    return order + [("own", 0)]


def scatter_steps(half, way, step):
    return {"a": half - step, "b": -(half - 1 - step), "own": 0}[way]


def add_rows(out, refs, rows):
    start, size = rows
    tile = min(size, 64)

    @pl.loop(0, size // tile)
    def _(i):
        where = pl.ds(pl.multiple_of(start + i * tile, tile), tile)
        total = refs[0][where, :].astype(jnp.float32)
        for ref in refs[1:]:
            total += ref[where, :].astype(jnp.float32)
        out[where, :] = total.astype(out.dtype)


def reduce_scatter(ring, by_dev, part, out, after, scratch):
    mine, theirs, from_a, from_b, local_sem, pair_send, pair_recv, a_send, a_recv, b_send, b_recv = scratch
    half = ring.half
    size = part.shape[1] // SPLIT
    order = order_of_use(half)
    to_a, to_b, sibling = ring.partners()
    copies, pairs = [], []
    for j, (way, step) in enumerate(order):
        steps = scatter_steps(half, way, step)
        pair = remote(
            part.at[ring.chunk(by_dev, -ring.sign * steps, 1)],
            theirs.at[j], pair_send.at[j], pair_recv.at[j], sibling,
        )
        pair.start()
        pairs.append(pair)
        copy = pltpu.make_async_copy(
            part.at[ring.chunk(by_dev, ring.sign * steps)], mine.at[j], local_sem.at[j]
        )
        copy.start()
        copies.append(copy)
    sent = {}
    for j, (way, step) in enumerate(order):
        copies[j].wait()
        pairs[j].wait_recv()
        for h in range(SPLIT):
            rows = pl.ds(h * size, size)
            refs = [mine.at[j], theirs.at[j]]
            if way == "own":
                sent["a", half - 1, h].wait_recv()
                refs.append(from_a.at[half - 1])
                if half > 1:
                    sent["b", half - 2, h].wait_recv()
                    refs.append(from_b.at[half - 2])
                add_rows(out, refs, (h * size, size))
                after(h)
                continue
            landing, send, recv, who = (
                (from_a, a_send, a_recv, to_a) if way == "a" else (from_b, b_send, b_recv, to_b)
            )
            if step:
                sent[way, step - 1, h].wait_recv()
                refs.append(landing.at[step - 1])
            add_rows(mine.at[j], refs, (h * size, size))
            copy = remote(
                mine.at[j, rows], landing.at[step, rows],
                send.at[step * SPLIT + h], recv.at[step * SPLIT + h], who,
            )
            copy.start()
            sent[way, step, h] = copy
    for copy in sent.values():
        copy.wait_send()
    for pair in pairs:
        pair.wait_send()


def scatter_scratch(chips, rows, columns):
    half = chips // 2
    dma = pltpu.SemaphoreType.DMA
    return [
        pltpu.VMEM((chips, rows, columns), jnp.bfloat16),
        pltpu.VMEM((chips, rows, columns), jnp.bfloat16),
        pltpu.VMEM((half, rows, columns), jnp.bfloat16),
        pltpu.VMEM((max(half - 1, 1), rows, columns), jnp.bfloat16),
        dma((chips,)), dma((chips,)), dma((chips,)),
        dma((half * SPLIT,)), dma((half * SPLIT,)), dma((half * SPLIT,)), dma((half * SPLIT,)),
    ]


class Gather:
    def __init__(self, ring, by_dev, own, full, scratch):
        self.ring, self.by_dev, self.own, self.full = ring, by_dev, own, full
        self.local_sem, self.sems = scratch[0], scratch[1:]
        self.size = own.shape[0] // SPLIT
        self.sent, self.started = {}, []

    def piece(self, steps, h):
        return self.full.at[self.ring.chunk(self.by_dev, steps), pl.ds(h * self.size, self.size)]

    def send(self, way, step, h):
        ring = self.ring
        steps = {"a": -step, "b": step, "p": -step, "q": step}[way]
        steps = ring.sign * steps
        dst = self.piece(steps, h)
        src = self.own.at[pl.ds(h * self.size, self.size)] if step == 0 else dst
        i = "abpq".index(way)
        who = ring.partners()[min(i, 2)]
        index = step * SPLIT + h
        copy = remote(src, dst, self.sems[2 * i].at[index], self.sems[2 * i + 1].at[index], who)
        copy.start()
        self.sent[way, step, h] = copy

    def start(self, h):
        copy = pltpu.make_async_copy(
            self.own.at[pl.ds(h * self.size, self.size)], self.piece(0, h), self.local_sem.at[h]
        )
        copy.start()
        self.started.append(copy)
        self.send("a", 0, h)
        if self.ring.half > 1:
            self.send("b", 0, h)
        self.send("p", 0, h)

    def finish(self):
        half = self.ring.half
        for step in range(1, half + 1):
            for h in range(SPLIT):
                self.sent["a", step - 1, h].wait_recv()
                if step < half:
                    self.send("a", step, h)
                self.send("p", step, h)
                if step < half:
                    self.sent["b", step - 1, h].wait_recv()
                    if step < half - 1:
                        self.send("b", step, h)
                    self.send("q", step, h)
        for copy in self.started:
            copy.wait()
        for (way, step, h), copy in self.sent.items():
            copy.wait_send()
            if way in "pq":
                copy.wait_recv()


def gather_scratch(chips):
    dma = pltpu.SemaphoreType.DMA
    return [dma((SPLIT,))] + [dma(((chips // 2 + 1) * SPLIT,))] * 8


def gather_kernel(reg, dev, own, full, *scratch):
    ring = Ring(reg, dev)
    ring.barrier()
    gather = Gather(ring, False, own, full, scratch)
    for h in range(SPLIT):
        gather.start(h)
    gather.finish()


def image_kernel(reg, dev, part, full, shard, *scratch):
    ring = Ring(reg, dev)
    ring.barrier()
    gather = Gather(ring, True, shard, full, scratch[11:])
    reduce_scatter(ring, True, part, shard, gather.start, scratch[:11])
    gather.finish()


def scatter_kernel(reg, dev, part, out, *scratch):
    ring = Ring(reg, dev)
    ring.barrier()
    reduce_scatter(ring, False, part, out, lambda h: None, scratch)


def remote_params(collective_id):
    return pltpu.CompilerParams(
        collective_id=collective_id, has_side_effects=True, vmem_limit_bytes=VMEM_LIMIT
    )


def multiply_kernel(transposed, order, keep, pos, take, blocks, table, out):
    count = blocks.shape[0]
    zero = jnp.zeros(out.shape[1:], out.dtype)

    @pl.loop(0, out.shape[0])
    def _(i):
        out[i] = zero

    contract = ((0,), (0,)) if transposed else ((1,), (0,))

    def step(i, total):
        term = lax.dot_general(
            blocks[order[i]], table[take[i]], (contract, ((), ())),
            preferred_element_type=jnp.float32,
        )
        total = jnp.where(keep[i] == 1, total, 0.0) + term
        out[pos[i]] = total.astype(out.dtype)
        return total

    lax.fori_loop(0, count, step, jnp.zeros(out.shape[1:], jnp.float32), unroll=4)


def multiply(transposed, plan, blocks, table, positions):
    count, cells, _ = blocks.shape
    rows, _, columns = table.shape
    held = (rows + positions) * cells * columns * 2
    pieces = 1 if held <= 40 * 2**20 else 2
    width = columns // pieces
    once = pl.Buffered(1)
    return pl.pallas_call(
        functools.partial(multiply_kernel, transposed),
        out_shape=jax.ShapeDtypeStruct((positions, cells, columns), jnp.bfloat16),
        grid_spec=pltpu.PrefetchScalarGridSpec(
            num_scalar_prefetch=4,
            grid=(pieces,),
            in_specs=[
                pl.BlockSpec((count, cells, cells), lambda i, *_: (0, 0, 0), pipeline_mode=once),
                pl.BlockSpec((rows, cells, width), lambda i, *_: (0, 0, i), pipeline_mode=once),
            ],
            out_specs=pl.BlockSpec((positions, cells, width), lambda i, *_: (0, 0, i), pipeline_mode=once),
        ),
        compiler_params=pltpu.CompilerParams(vmem_limit_bytes=VMEM_LIMIT),
    )(*plan, blocks, table)


def look_up(place, index):
    hit = index[:, None] == jnp.arange(place.shape[0], dtype=jnp.int32)[None, :]
    return jnp.sum(jnp.where(hit, place[None, :], 0), axis=1)


def sorted_plan(pos, take):
    count = pos.shape[0]
    number = jnp.arange(count, dtype=jnp.int32)
    key = pos * count + number
    rank = jnp.sum((key[None, :] < key[:, None]).astype(jnp.int32), axis=1)
    hit = rank[None, :] == number[:, None]
    pick = lambda values: jnp.sum(jnp.where(hit, values[None, :], 0), axis=1)
    pos_sorted = pick(pos)
    before = jnp.concatenate([jnp.full((1,), -1, jnp.int32), pos_sorted[:-1]])
    return pick(number), (pos_sorted == before).astype(jnp.int32), pos_sorted, pick(take)


def local(footprints, block_coords, receptor_place, source_place, probe_matrix):
    cells = footprints.shape[1]
    columns = probe_matrix.shape[1]
    reg, dev = lax.axis_size("reg"), lax.axis_size("dev")
    chips, devices = reg // 2 * dev, reg * dev
    receptors = receptor_place.shape[0]
    sources = probe_matrix.shape[0] * devices // cells
    bf16 = jnp.bfloat16

    pos_rec = look_up(receptor_place, block_coords[:, 0])
    pos_src = look_up(source_place, block_coords[:, 1])
    forward_plan = sorted_plan(pos_rec, pos_src)
    backward_plan = sorted_plan(pos_src, pos_rec)

    probe_rows = probe_matrix.shape[0]
    probe = pl.pallas_call(
        functools.partial(gather_kernel, reg, dev),
        out_shape=jax.ShapeDtypeStruct((devices, probe_rows, columns), bf16),
        in_specs=[ANY], out_specs=ANY,
        scratch_shapes=gather_scratch(chips),
        compiler_params=remote_params(1),
    )(probe_matrix)

    receptor_part = multiply(False, forward_plan, footprints, probe.reshape(sources, cells, columns), receptors)

    image_rows = receptors * cells // devices
    image = pl.pallas_call(
        functools.partial(image_kernel, reg, dev),
        out_shape=jax.ShapeDtypeStruct((devices, image_rows, columns), bf16),
        in_specs=[ANY], out_specs=ANY,
        scratch_shapes=[pltpu.VMEM((image_rows, columns), bf16)]
        + scatter_scratch(chips, image_rows, columns) + gather_scratch(chips),
        compiler_params=remote_params(2),
    )(receptor_part.reshape(devices, image_rows, columns))
    receptor_image = lax.dynamic_slice_in_dim(image, lax.axis_index("dev") * reg, reg, 0)

    source_part = multiply(True, backward_plan, footprints, image.reshape(receptors, cells, columns), sources)

    source_image = pl.pallas_call(
        functools.partial(scatter_kernel, reg, dev),
        out_shape=jax.ShapeDtypeStruct((probe_rows, columns), jnp.float32),
        in_specs=[ANY], out_specs=pl.BlockSpec(memory_space=pltpu.VMEM),
        scratch_shapes=scatter_scratch(chips, probe_rows, columns),
        compiler_params=remote_params(3),
    )(source_part.reshape(devices, probe_rows, columns))
    return receptor_image.reshape(reg * image_rows, columns), source_image


def solution(mesh):
    return jax.shard_map(
        local,
        mesh=mesh,
        in_specs=(
            P(("grp", "reg", "dev"), None, None),
            P(("grp", "reg", "dev"), None),
            P("grp"),
            P("grp"),
            P(("grp", "reg", "dev"), None),
        ),
        out_specs=(P(("grp", "dev"), None), P(("grp", "reg", "dev"), None)),
        check_vma=False,
    )
```

```python
import functools

import jax
import jax.numpy as jnp
from jax import lax
from jax.experimental import pallas as pl
from jax.experimental.pallas import tpu as pltpu
from jax.sharding import PartitionSpec as P

MESH = pl.DeviceIdType.MESH
ANY = pl.BlockSpec(memory_space=pl.ANY)
VMEM_LIMIT = 60 * 2**20
SPLIT = 2
SLICES = 16
AHEAD = 3


class Ring:
    def __init__(self, reg, dev):
        self.reg, self.dev = reg, dev
        self.chips = reg // 2 * dev
        self.half = self.chips // 2
        r, z = lax.axis_index("reg"), lax.axis_index("dev")
        x, self.core = r // 2, r % 2
        self.at = x * dev + z + (x % 2) * (dev - 1 - 2 * z)
        self.sign = 1 - 2 * self.core

    def place(self, steps):
        at = lax.rem(self.at + steps + 2 * self.chips, self.chips)
        x, z = at // self.dev, at % self.dev
        return x, z + (x % 2) * (self.dev - 1 - 2 * z)

    def device(self, steps, other=0):
        x, z = self.place(steps)
        return {"reg": 2 * x + (self.core if not other else 1 - self.core), "dev": z}

    def chunk(self, by_dev, steps, other=0):
        x, z = self.place(steps)
        r = 2 * x + (self.core if not other else 1 - self.core)
        return z * self.reg + r if by_dev else r * self.dev + z

    def partners(self):
        return self.device(self.sign), self.device(-self.sign), self.device(0, 1)

    def barrier(self):
        barrier = pltpu.get_barrier_semaphore()
        for who in self.partners():
            pl.semaphore_signal(barrier, inc=1, device_id=who, device_id_type=MESH)
        pl.semaphore_wait(barrier, 3)


def remote(src, dst, send, recv, who):
    return pltpu.make_async_remote_copy(
        src_ref=src, dst_ref=dst, send_sem=send, recv_sem=recv, device_id=who, device_id_type=MESH
    )


def order_of_use(half):
    order = []
    for step in range(half):
        order.append(("a", step))
        if step < half - 1:
            order.append(("b", step))
    return order + [("own", 0)]


def scatter_steps(half, way, step):
    return {"a": half - step, "b": -(half - 1 - step), "own": 0}[way]


def add_rows(out, refs, rows):
    start, size = rows
    tile = min(size, 64)

    @pl.loop(0, size // tile)
    def _(i):
        where = pl.ds(pl.multiple_of(start + i * tile, tile), tile)
        total = refs[0][where, :].astype(jnp.float32)
        for ref in refs[1:]:
            total += ref[where, :].astype(jnp.float32)
        out[where, :] = total.astype(out.dtype)


def reduce_scatter(ring, by_dev, part, out, after, scratch):
    mine, theirs, from_a, from_b, local_sem, pair_send, pair_recv, a_send, a_recv, b_send, b_recv = scratch
    half = ring.half
    size = part.shape[1] // SPLIT
    order = order_of_use(half)
    to_a, to_b, sibling = ring.partners()
    copies, pairs = [], []
    for j, (way, step) in enumerate(order):
        steps = scatter_steps(half, way, step)
        pair = remote(
            part.at[ring.chunk(by_dev, -ring.sign * steps, 1)],
            theirs.at[j], pair_send.at[j], pair_recv.at[j], sibling,
        )
        pair.start()
        pairs.append(pair)
        copy = pltpu.make_async_copy(
            part.at[ring.chunk(by_dev, ring.sign * steps)], mine.at[j], local_sem.at[j]
        )
        copy.start()
        copies.append(copy)
    sent = {}
    for j, (way, step) in enumerate(order):
        copies[j].wait()
        pairs[j].wait_recv()
        for h in range(SPLIT):
            rows = pl.ds(h * size, size)
            refs = [mine.at[j], theirs.at[j]]
            if way == "own":
                sent["a", half - 1, h].wait_recv()
                refs.append(from_a.at[half - 1])
                if half > 1:
                    sent["b", half - 2, h].wait_recv()
                    refs.append(from_b.at[half - 2])
                add_rows(out, refs, (h * size, size))
                after(h)
                continue
            landing, send, recv, who = (
                (from_a, a_send, a_recv, to_a) if way == "a" else (from_b, b_send, b_recv, to_b)
            )
            if step:
                sent[way, step - 1, h].wait_recv()
                refs.append(landing.at[step - 1])
            add_rows(mine.at[j], refs, (h * size, size))
            copy = remote(
                mine.at[j, rows], landing.at[step, rows],
                send.at[step * SPLIT + h], recv.at[step * SPLIT + h], who,
            )
            copy.start()
            sent[way, step, h] = copy
    for copy in sent.values():
        copy.wait_send()
    for pair in pairs:
        pair.wait_send()


def scatter_scratch(chips, rows, columns):
    half = chips // 2
    dma = pltpu.SemaphoreType.DMA
    return [
        pltpu.VMEM((chips, rows, columns), jnp.bfloat16),
        pltpu.VMEM((chips, rows, columns), jnp.bfloat16),
        pltpu.VMEM((half, rows, columns), jnp.bfloat16),
        pltpu.VMEM((max(half - 1, 1), rows, columns), jnp.bfloat16),
        dma((chips,)), dma((chips,)), dma((chips,)),
        dma((half * SPLIT,)), dma((half * SPLIT,)), dma((half * SPLIT,)), dma((half * SPLIT,)),
    ]


class Gather:
    def __init__(self, ring, by_dev, own, full, scratch):
        self.ring, self.by_dev, self.own, self.full = ring, by_dev, own, full
        self.local_sem, self.sems = scratch[0], scratch[1:]
        self.size = own.shape[0] // SPLIT
        self.sent, self.started = {}, []

    def piece(self, steps, h):
        return self.full.at[self.ring.chunk(self.by_dev, steps), pl.ds(h * self.size, self.size)]

    def send(self, way, step, h):
        ring = self.ring
        steps = {"a": -step, "b": step, "p": -step, "q": step}[way]
        steps = ring.sign * steps
        dst = self.piece(steps, h)
        src = self.own.at[pl.ds(h * self.size, self.size)] if step == 0 else dst
        i = "abpq".index(way)
        who = ring.partners()[min(i, 2)]
        index = step * SPLIT + h
        copy = remote(src, dst, self.sems[2 * i].at[index], self.sems[2 * i + 1].at[index], who)
        copy.start()
        self.sent[way, step, h] = copy

    def start(self, h):
        copy = pltpu.make_async_copy(
            self.own.at[pl.ds(h * self.size, self.size)], self.piece(0, h), self.local_sem.at[h]
        )
        copy.start()
        self.started.append(copy)
        self.send("a", 0, h)
        if self.ring.half > 1:
            self.send("b", 0, h)
        self.send("p", 0, h)

    def finish(self):
        half = self.ring.half
        for step in range(1, half + 1):
            for h in range(SPLIT):
                self.sent["a", step - 1, h].wait_recv()
                if step < half:
                    self.send("a", step, h)
                self.send("p", step, h)
                if step < half:
                    self.sent["b", step - 1, h].wait_recv()
                    if step < half - 1:
                        self.send("b", step, h)
                    self.send("q", step, h)
        for copy in self.started:
            copy.wait()
        for (way, step, h), copy in self.sent.items():
            copy.wait_send()
            if way in "pq":
                copy.wait_recv()


def gather_scratch(chips):
    dma = pltpu.SemaphoreType.DMA
    return [dma((SPLIT,))] + [dma(((chips // 2 + 1) * SPLIT,))] * 8


def gather_kernel(reg, dev, own, full, *scratch):
    ring = Ring(reg, dev)
    ring.barrier()
    gather = Gather(ring, False, own, full, scratch)
    for h in range(SPLIT):
        gather.start(h)
    gather.finish()


def image_kernel(reg, dev, part, full, shard, *scratch):
    ring = Ring(reg, dev)
    ring.barrier()
    gather = Gather(ring, True, shard, full, scratch[11:])
    reduce_scatter(ring, True, part, shard, gather.start, scratch[:11])
    gather.finish()


def scatter_kernel(reg, dev, part, out, *scratch):
    ring = Ring(reg, dev)
    ring.barrier()
    reduce_scatter(ring, False, part, out, lambda h: None, scratch)


def remote_params(collective_id):
    return pltpu.CompilerParams(
        collective_id=collective_id, has_side_effects=True, vmem_limit_bytes=VMEM_LIMIT
    )


def multiply_kernel(transposed, order, keep, pos, take, blocks, table, out):
    count = blocks.shape[0]
    zero = jnp.zeros(out.shape[1:], out.dtype)

    @pl.loop(0, out.shape[0])
    def _(i):
        out[i] = zero

    contract = ((0,), (0,)) if transposed else ((1,), (0,))

    def step(i, total):
        term = lax.dot_general(
            blocks[order[i]], table[take[i]], (contract, ((), ())),
            preferred_element_type=jnp.float32,
        )
        total = jnp.where(keep[i] == 1, total, 0.0) + term
        out[pos[i]] = total.astype(out.dtype)
        return total

    lax.fori_loop(0, count, step, jnp.zeros(out.shape[1:], jnp.float32), unroll=4)


def multiply(transposed, plan, blocks, table, positions):
    count, cells, _ = blocks.shape
    rows, _, columns = table.shape
    held = (rows + positions) * cells * columns * 2
    pieces = 1 if held <= 40 * 2**20 else 2
    width = columns // pieces
    once = pl.Buffered(1)
    return pl.pallas_call(
        functools.partial(multiply_kernel, transposed),
        out_shape=jax.ShapeDtypeStruct((positions, cells, columns), jnp.bfloat16),
        grid_spec=pltpu.PrefetchScalarGridSpec(
            num_scalar_prefetch=4,
            grid=(pieces,),
            in_specs=[
                pl.BlockSpec((count, cells, cells), lambda i, *_: (0, 0, 0), pipeline_mode=once),
                pl.BlockSpec((rows, cells, width), lambda i, *_: (0, 0, i), pipeline_mode=once),
            ],
            out_specs=pl.BlockSpec((positions, cells, width), lambda i, *_: (0, 0, i), pipeline_mode=once),
        ),
        compiler_params=pltpu.CompilerParams(vmem_limit_bytes=VMEM_LIMIT),
    )(*plan, blocks, table)


class HalfGather:
    def __init__(self, ring, by_dev, full, scratch):
        self.ring, self.by_dev, self.full, self.sems = ring, by_dev, full, scratch
        self.blocks = full.shape[0] // (2 * ring.chips)
        self.size = self.blocks // SPLIT
        self.sent = {}

    def send(self, way, step, h):
        ring = self.ring
        steps = ring.sign * {"a": -step, "b": step, "p": -step, "q": step}[way]
        first = ring.chunk(self.by_dev, steps) * self.blocks + h * self.size
        piece = self.full.at[pl.ds(first, self.size)]
        i = "abpq".index(way)
        index = step * SPLIT + h
        copy = remote(
            piece, piece, self.sems[2 * i].at[index], self.sems[2 * i + 1].at[index],
            ring.partners()[min(i, 2)],
        )
        copy.start()
        self.sent[way, step, h] = copy

    def start(self, h):
        self.send("a", 0, h)
        if self.ring.half > 1:
            self.send("b", 0, h)
        self.send("p", 0, h)

    def step(self, step, work):
        half = self.ring.half
        for h in range(SPLIT):
            work()
            self.sent["a", step - 1, h].wait_recv()
            if step < half:
                self.send("a", step, h)
            self.send("p", step, h)
            if step < half:
                work()
                self.sent["b", step - 1, h].wait_recv()
                if step < half - 1:
                    self.send("b", step, h)
                self.send("q", step, h)

    def advance(self, work):
        for step in range(1, self.ring.half):
            self.step(step, work)

    def tail(self):
        self.step(self.ring.half, lambda: None)
        for (way, step, h), copy in self.sent.items():
            if way in "pq":
                copy.wait_recv()

    def drain(self):
        for copy in self.sent.values():
            copy.wait_send()


class HalfScatter:
    def __init__(self, ring, by_dev, part, scratch):
        self.ring, self.by_dev, self.part = ring, by_dev, part
        self.theirs, self.from_a, self.from_b = scratch[:3]
        self.pair_send, self.pair_recv, self.a_send, self.a_recv, self.b_send, self.b_recv = scratch[3:]
        self.order = order_of_use(ring.half)
        self.blocks = part.shape[0] // (2 * ring.chips)
        self.size = self.blocks // SPLIT
        self.pairs, self.sent = [], {}

    def pair(self):
        j = len(self.pairs)
        if j == len(self.order):
            return
        ring = self.ring
        steps = scatter_steps(ring.half, *self.order[j])
        first = ring.chunk(self.by_dev, -ring.sign * steps, 1) * self.blocks
        copy = remote(
            self.part.at[pl.ds(first, self.blocks)], self.theirs.at[pl.ds(j * self.blocks, self.blocks)],
            self.pair_send.at[j], self.pair_recv.at[j], ring.device(0, 1),
        )
        copy.start()
        self.pairs.append(copy)

    def chunk(self, j, work, store, after):
        ring, half = self.ring, self.ring.half
        way, step = self.order[j]
        work()
        self.pairs[j].wait_recv()
        self.pair()
        to_a, to_b, _ = ring.partners()
        for h in range(SPLIT):
            first = ring.chunk(self.by_dev, ring.sign * scatter_steps(half, way, step)) * self.blocks
            mine = self.part.at[pl.ds(first + h * self.size, self.size)]
            refs = [mine, self.theirs.at[pl.ds(j * self.blocks + h * self.size, self.size)]]
            before = [("a", half - 1), ("b", half - 2)] if way == "own" else [(way, step - 1)]
            for w, s in before:
                if s >= 0:
                    work()
                    self.sent[w, s, h].wait_recv()
                    landing = self.from_a if w == "a" else self.from_b
                    refs.append(landing.at[pl.ds(s * self.blocks + h * self.size, self.size)])
            put = (lambda i, v: store(h * self.size + i, v)) if way == "own" else None

            @pl.loop(0, self.size)
            def _(i):
                total = refs[0][i].astype(jnp.float32)
                for ref in refs[1:]:
                    total += ref[i].astype(jnp.float32)
                if put is None:
                    mine[i] = total.astype(mine.dtype)
                else:
                    put(i, total)

            if way == "own":
                after(h)
                continue
            landing, send, recv, who = (
                (self.from_a, self.a_send, self.a_recv, to_a)
                if way == "a"
                else (self.from_b, self.b_send, self.b_recv, to_b)
            )
            copy = remote(
                mine, landing.at[pl.ds(step * self.blocks + h * self.size, self.size)],
                send.at[step * SPLIT + h], recv.at[step * SPLIT + h], who,
            )
            copy.start()
            self.sent[way, step, h] = copy

    def start(self):
        for _ in range(AHEAD):
            self.pair()
        for j in range(len(self.order)):
            if self.order[j][1] == 0 and self.order[j][0] != "own":
                self.chunk(j, lambda: None, None, None)

    def advance(self, work):
        for j in range(len(self.order) - 1):
            if self.order[j][1] > 0:
                self.chunk(j, work, None, None)

    def final(self, store, after=lambda h: None):
        self.chunk(len(self.order) - 1, lambda: None, store, after)

    def drain(self):
        for copy in [*self.sent.values(), *self.pairs]:
            copy.wait_send()


class Job:
    def __init__(self, transposed, plan, blocks, table, running, total, part):
        self.order, self.keep, self.take, self.last = plan
        self.blocks, self.table, self.running, self.total, self.part = blocks, table, running, total, part
        self.contract = ((0,), (0,)) if transposed else ((1,), (0,))
        self.done = 0
        self.size = blocks.shape[0] // SLICES

    def slice(self):
        if self.done == SLICES:
            return
        start = self.done * self.size
        self.done += 1

        def step(i, total):
            term = lax.dot_general(
                self.blocks[self.order[start + i]], self.table[self.take[start + i]],
                (self.contract, ((), ())), preferred_element_type=jnp.float32,
            )
            total = jnp.where(self.keep[start + i] == 1, total, 0.0) + term
            self.running[start + i] = total.astype(self.running.dtype)
            return total

        self.total[...] = lax.fori_loop(0, self.size, step, self.total[...], unroll=min(4, self.size))

    def finish(self):
        while self.done < SLICES:
            self.slice()

        def place(p, unused):
            self.part[p] = self.running[self.last[p]]
            return unused

        lax.fori_loop(0, self.part.shape[0], place, 0, unroll=2)


def fused_kernel(reg, dev, *refs):
    forward_plan, backward_plan, refs = refs[:4], refs[4:8], refs[8:]
    (footprints, probe_matrix, image_out, source_out), refs = refs[:4], refs[4:]
    blocks, probe, image, part, source_part = refs[0], refs[1:3], refs[3:5], refs[5:7], refs[7:9]
    running, total, blocks_sem, probe_sem, image_sem = refs[9:14]
    refs = refs[14:]
    gathers, scatters = [refs[8 * i : 8 * i + 8] for i in range(4)], [refs[32 + 9 * i : 41 + 9 * i] for i in range(4)]
    idle = lambda: None
    ring = Ring(reg, dev)
    cells = blocks.shape[1]
    own_probe = ring.chunk(False, 0) * (probe_matrix.shape[0] // cells)
    own_image = ring.chunk(True, 0) * (image[0].shape[0] // (2 * ring.chips))
    width = probe_matrix.shape[1] // 2
    loads = []
    for h in range(2):
        for b in range(probe_matrix.shape[0] // cells):
            copy = pltpu.make_async_copy(
                probe_matrix.at[pl.ds(b * cells, cells), pl.ds(h * width, width)],
                probe[h].at[own_probe + b], probe_sem.at[h, b],
            )
            copy.start()
            loads.append(copy)
    load_blocks = pltpu.make_async_copy(footprints, blocks, blocks_sem)
    load_blocks.start()
    ring.barrier()
    for copy in loads:
        copy.wait()
    running[running.shape[0] - 1] = jnp.zeros(running.shape[1:], running.dtype)
    total[...] = jnp.zeros_like(total)

    spread = [HalfGather(ring, False, probe[h], gathers[h]) for h in range(2)]
    forward = [Job(False, forward_plan, blocks, probe[h], running, total, part[h]) for h in range(2)]
    gather = [HalfGather(ring, True, image[h], gathers[2 + h]) for h in range(2)]
    scatter = [HalfScatter(ring, True, part[h], scatters[h]) for h in range(2)]
    backward = [Job(True, backward_plan, blocks, image[h], running, total, source_part[h]) for h in range(2)]
    collect = [HalfScatter(ring, False, source_part[h], scatters[2 + h]) for h in range(2)]

    def start_all(phase):
        for h in range(SPLIT):
            phase.start(h)

    def keep_image(h):
        def store(i, value):
            image[h][own_image + i] = value.astype(image[h].dtype)
        return store

    def keep_source(h):
        def store(i, value):
            source_out[pl.ds(pl.multiple_of(i * cells, cells), cells), h * width : (h + 1) * width] = value
        return store

    outs = []

    def write_image(h):
        count = image_out.shape[0] // cells
        first = lax.axis_index("dev") * count
        for b in range(count):
            copy = pltpu.make_async_copy(
                image[h].at[first + b],
                image_out.at[pl.ds(b * cells, cells), pl.ds(h * width, width)], image_sem.at[h, b],
            )
            copy.start()
            outs.append(copy)

    start_all(spread[0])
    spread[0].advance(idle)
    start_all(spread[1])
    spread[0].tail()
    load_blocks.wait()
    spread[1].advance(forward[0].slice)
    forward[0].finish()
    scatter[0].start()
    spread[1].tail()
    scatter[0].advance(forward[1].slice)
    forward[1].finish()
    scatter[1].start()
    scatter[0].final(keep_image(0))
    scatter[1].advance(idle)
    start_all(gather[0])
    scatter[1].final(keep_image(1))
    gather[0].advance(idle)
    start_all(gather[1])
    gather[0].tail()
    write_image(0)
    gather[1].advance(backward[0].slice)
    backward[0].finish()
    collect[0].start()
    gather[1].tail()
    write_image(1)
    collect[0].advance(backward[1].slice)
    backward[1].finish()
    collect[1].start()
    collect[0].final(keep_source(0))
    collect[1].advance(idle)
    collect[1].final(keep_source(1))
    for phase in (*spread, *scatter, *gather, *collect):
        phase.drain()
    for copy in outs:
        copy.wait()


def half_scatter_scratch(chips, blocks, cells, width):
    half = chips // 2
    dma = pltpu.SemaphoreType.DMA
    buffer = lambda n: pltpu.VMEM((n * blocks, cells, width), jnp.bfloat16)
    return [buffer(chips), buffer(half), buffer(max(half - 1, 1)), dma((chips,)), dma((chips,))] + [
        dma((half * SPLIT,))
    ] * 4


def fused(reg, dev, forward_plan, backward_plan, footprints, probe_matrix, receptors):
    count, cells, _ = footprints.shape
    chips, devices = reg // 2 * dev, reg * dev
    width = probe_matrix.shape[1] // 2
    own_sources, own_receptors = probe_matrix.shape[0] // cells, receptors // devices
    sources = own_sources * devices
    buffer = lambda n: pltpu.VMEM((n, cells, width), jnp.bfloat16)
    dma = pltpu.SemaphoreType.DMA
    scratch = (
        [pltpu.VMEM(footprints.shape, jnp.bfloat16)]
        + [buffer(sources)] * 2 + [buffer(receptors)] * 4 + [buffer(sources)] * 2
        + [buffer(count + 1), pltpu.VMEM((cells, width), jnp.float32)]
        + [dma(()), dma((2, own_sources)), dma((2, own_receptors * reg))]
        + gather_scratch(chips)[1:] * 4
        + half_scatter_scratch(chips, own_receptors, cells, width) * 2
        + half_scatter_scratch(chips, own_sources, cells, width) * 2
    )
    return pl.pallas_call(
        functools.partial(fused_kernel, reg, dev),
        out_shape=(
            jax.ShapeDtypeStruct((receptors // dev * cells, 2 * width), jnp.bfloat16),
            jax.ShapeDtypeStruct(probe_matrix.shape, jnp.float32),
        ),
        in_specs=[pl.BlockSpec(memory_space=pltpu.SMEM)] * 8 + [ANY] * 2,
        out_specs=(ANY, pl.BlockSpec(memory_space=pltpu.VMEM)),
        scratch_shapes=scratch,
        compiler_params=remote_params(4),
    )(*forward_plan, *backward_plan, footprints, probe_matrix)


def with_last(plan, positions):
    order, keep, pos, take = plan
    hit = pos[None, :] == jnp.arange(positions, dtype=jnp.int32)[:, None]
    place = jnp.max(jnp.where(hit, jnp.arange(pos.shape[0], dtype=jnp.int32)[None, :], -1), axis=1)
    return order, keep, take, jnp.where(place < 0, pos.shape[0], place)


def look_up(place, index):
    hit = index[:, None] == jnp.arange(place.shape[0], dtype=jnp.int32)[None, :]
    return jnp.sum(jnp.where(hit, place[None, :], 0), axis=1)


def sorted_plan(pos, take):
    count = pos.shape[0]
    number = jnp.arange(count, dtype=jnp.int32)
    key = pos * count + number
    rank = jnp.sum((key[None, :] < key[:, None]).astype(jnp.int32), axis=1)
    hit = rank[None, :] == number[:, None]
    pick = lambda values: jnp.sum(jnp.where(hit, values[None, :], 0), axis=1)
    pos_sorted = pick(pos)
    before = jnp.concatenate([jnp.full((1,), -1, jnp.int32), pos_sorted[:-1]])
    return pick(number), (pos_sorted == before).astype(jnp.int32), pos_sorted, pick(take)


def local(footprints, block_coords, receptor_place, source_place, probe_matrix):
    cells = footprints.shape[1]
    columns = probe_matrix.shape[1]
    reg, dev = lax.axis_size("reg"), lax.axis_size("dev")
    chips, devices = reg // 2 * dev, reg * dev
    receptors = receptor_place.shape[0]
    sources = probe_matrix.shape[0] * devices // cells
    bf16 = jnp.bfloat16

    pos_rec = look_up(receptor_place, block_coords[:, 0])
    pos_src = look_up(source_place, block_coords[:, 1])
    forward_plan = sorted_plan(pos_rec, pos_src)
    backward_plan = sorted_plan(pos_src, pos_rec)

    block_bytes = 2 * cells * columns // 2
    blocks_held = 2 * (3 * receptors + 3 * sources) + 2 * footprints.shape[0]
    divides = columns % 256 == 0 and footprints.shape[0] % SLICES == 0
    if blocks_held * block_bytes <= 48 * 2**20 and divides and chips >= 4:
        return fused(
            reg, dev, with_last(forward_plan, receptors), with_last(backward_plan, sources),
            footprints, probe_matrix, receptors,
        )

    probe_rows = probe_matrix.shape[0]
    probe = pl.pallas_call(
        functools.partial(gather_kernel, reg, dev),
        out_shape=jax.ShapeDtypeStruct((devices, probe_rows, columns), bf16),
        in_specs=[ANY], out_specs=ANY,
        scratch_shapes=gather_scratch(chips),
        compiler_params=remote_params(1),
    )(probe_matrix)

    receptor_part = multiply(False, forward_plan, footprints, probe.reshape(sources, cells, columns), receptors)

    image_rows = receptors * cells // devices
    image = pl.pallas_call(
        functools.partial(image_kernel, reg, dev),
        out_shape=jax.ShapeDtypeStruct((devices, image_rows, columns), bf16),
        in_specs=[ANY], out_specs=ANY,
        scratch_shapes=[pltpu.VMEM((image_rows, columns), bf16)]
        + scatter_scratch(chips, image_rows, columns) + gather_scratch(chips),
        compiler_params=remote_params(2),
    )(receptor_part.reshape(devices, image_rows, columns))
    receptor_image = lax.dynamic_slice_in_dim(image, lax.axis_index("dev") * reg, reg, 0)

    source_part = multiply(True, backward_plan, footprints, image.reshape(receptors, cells, columns), sources)

    source_image = pl.pallas_call(
        functools.partial(scatter_kernel, reg, dev),
        out_shape=jax.ShapeDtypeStruct((probe_rows, columns), jnp.float32),
        in_specs=[ANY], out_specs=pl.BlockSpec(memory_space=pltpu.VMEM),
        scratch_shapes=scatter_scratch(chips, probe_rows, columns),
        compiler_params=remote_params(3),
    )(source_part.reshape(devices, probe_rows, columns))
    return receptor_image.reshape(reg * image_rows, columns), source_image


def solution(mesh):
    return jax.shard_map(
        local,
        mesh=mesh,
        in_specs=(
            P(("grp", "reg", "dev"), None, None),
            P(("grp", "reg", "dev"), None),
            P("grp"),
            P("grp"),
            P(("grp", "reg", "dev"), None),
        ),
        out_specs=(P(("grp", "dev"), None), P(("grp", "reg", "dev"), None)),
        check_vma=False,
    )
```

```python
import functools

import jax
import jax.numpy as jnp
from jax import lax
from jax.experimental import pallas as pl
from jax.experimental.pallas import tpu as pltpu
from jax.sharding import PartitionSpec as P

MESH = pl.DeviceIdType.MESH
ANY = pl.BlockSpec(memory_space=pl.ANY)
VMEM_LIMIT = 60 * 2**20
SPLIT = 2
PIECES = 4
SLICES = 16
AHEAD = 3


class Ring:
    def __init__(self, reg, dev):
        self.reg, self.dev = reg, dev
        self.chips = reg // 2 * dev
        self.half = self.chips // 2
        r, z = lax.axis_index("reg"), lax.axis_index("dev")
        x, self.core = r // 2, r % 2
        self.at = x * dev + z + (x % 2) * (dev - 1 - 2 * z)
        self.sign = 1 - 2 * self.core

    def place(self, steps):
        at = lax.rem(self.at + steps + 2 * self.chips, self.chips)
        x, z = at // self.dev, at % self.dev
        return x, z + (x % 2) * (self.dev - 1 - 2 * z)

    def device(self, steps, other=0):
        x, z = self.place(steps)
        return {"reg": 2 * x + (self.core if not other else 1 - self.core), "dev": z}

    def chunk(self, by_dev, steps, other=0):
        x, z = self.place(steps)
        r = 2 * x + (self.core if not other else 1 - self.core)
        return z * self.reg + r if by_dev else r * self.dev + z

    def partners(self):
        return self.device(self.sign), self.device(-self.sign), self.device(0, 1)

    def barrier(self):
        barrier = pltpu.get_barrier_semaphore()
        for who in self.partners():
            pl.semaphore_signal(barrier, inc=1, device_id=who, device_id_type=MESH)
        pl.semaphore_wait(barrier, 3)


def remote(src, dst, send, recv, who):
    return pltpu.make_async_remote_copy(
        src_ref=src, dst_ref=dst, send_sem=send, recv_sem=recv, device_id=who, device_id_type=MESH
    )


def order_of_use(half):
    order = []
    for step in range(half):
        order.append(("a", step))
        if step < half - 1:
            order.append(("b", step))
    return order + [("own", 0)]


def scatter_steps(half, way, step):
    return {"a": half - step, "b": -(half - 1 - step), "own": 0}[way]


def add_rows(out, refs, rows):
    start, size = rows
    tile = min(size, 64)

    @pl.loop(0, size // tile)
    def _(i):
        where = pl.ds(pl.multiple_of(start + i * tile, tile), tile)
        total = refs[0][where, :].astype(jnp.float32)
        for ref in refs[1:]:
            total += ref[where, :].astype(jnp.float32)
        out[where, :] = total.astype(out.dtype)


def reduce_scatter(ring, by_dev, part, out, after, scratch):
    mine, theirs, from_a, from_b, local_sem, pair_send, pair_recv, a_send, a_recv, b_send, b_recv = scratch
    half = ring.half
    size = part.shape[1] // SPLIT
    order = order_of_use(half)
    to_a, to_b, sibling = ring.partners()
    copies, pairs = [], []
    for j, (way, step) in enumerate(order):
        steps = scatter_steps(half, way, step)
        pair = remote(
            part.at[ring.chunk(by_dev, -ring.sign * steps, 1)],
            theirs.at[j], pair_send.at[j], pair_recv.at[j], sibling,
        )
        pair.start()
        pairs.append(pair)
        copy = pltpu.make_async_copy(
            part.at[ring.chunk(by_dev, ring.sign * steps)], mine.at[j], local_sem.at[j]
        )
        copy.start()
        copies.append(copy)
    sent = {}
    for j, (way, step) in enumerate(order):
        copies[j].wait()
        pairs[j].wait_recv()
        for h in range(SPLIT):
            rows = pl.ds(h * size, size)
            refs = [mine.at[j], theirs.at[j]]
            if way == "own":
                sent["a", half - 1, h].wait_recv()
                refs.append(from_a.at[half - 1])
                if half > 1:
                    sent["b", half - 2, h].wait_recv()
                    refs.append(from_b.at[half - 2])
                add_rows(out, refs, (h * size, size))
                after(h)
                continue
            landing, send, recv, who = (
                (from_a, a_send, a_recv, to_a) if way == "a" else (from_b, b_send, b_recv, to_b)
            )
            if step:
                sent[way, step - 1, h].wait_recv()
                refs.append(landing.at[step - 1])
            add_rows(mine.at[j], refs, (h * size, size))
            copy = remote(
                mine.at[j, rows], landing.at[step, rows],
                send.at[step * SPLIT + h], recv.at[step * SPLIT + h], who,
            )
            copy.start()
            sent[way, step, h] = copy
    for copy in sent.values():
        copy.wait_send()
    for pair in pairs:
        pair.wait_send()


def scatter_scratch(chips, rows, columns):
    half = chips // 2
    dma = pltpu.SemaphoreType.DMA
    return [
        pltpu.VMEM((chips, rows, columns), jnp.bfloat16),
        pltpu.VMEM((chips, rows, columns), jnp.bfloat16),
        pltpu.VMEM((half, rows, columns), jnp.bfloat16),
        pltpu.VMEM((max(half - 1, 1), rows, columns), jnp.bfloat16),
        dma((chips,)), dma((chips,)), dma((chips,)),
        dma((half * SPLIT,)), dma((half * SPLIT,)), dma((half * SPLIT,)), dma((half * SPLIT,)),
    ]


class Gather:
    def __init__(self, ring, by_dev, own, full, scratch):
        self.ring, self.by_dev, self.own, self.full = ring, by_dev, own, full
        self.local_sem, self.sems = scratch[0], scratch[1:]
        self.size = own.shape[0] // SPLIT
        self.sent, self.started = {}, []

    def piece(self, steps, h):
        return self.full.at[self.ring.chunk(self.by_dev, steps), pl.ds(h * self.size, self.size)]

    def send(self, way, step, h):
        ring = self.ring
        steps = {"a": -step, "b": step, "p": -step, "q": step}[way]
        steps = ring.sign * steps
        dst = self.piece(steps, h)
        src = self.own.at[pl.ds(h * self.size, self.size)] if step == 0 else dst
        i = "abpq".index(way)
        who = ring.partners()[min(i, 2)]
        index = step * SPLIT + h
        copy = remote(src, dst, self.sems[2 * i].at[index], self.sems[2 * i + 1].at[index], who)
        copy.start()
        self.sent[way, step, h] = copy

    def start(self, h):
        copy = pltpu.make_async_copy(
            self.own.at[pl.ds(h * self.size, self.size)], self.piece(0, h), self.local_sem.at[h]
        )
        copy.start()
        self.started.append(copy)
        self.send("a", 0, h)
        if self.ring.half > 1:
            self.send("b", 0, h)
        self.send("p", 0, h)

    def finish(self):
        half = self.ring.half
        for step in range(1, half + 1):
            for h in range(SPLIT):
                self.sent["a", step - 1, h].wait_recv()
                if step < half:
                    self.send("a", step, h)
                self.send("p", step, h)
                if step < half:
                    self.sent["b", step - 1, h].wait_recv()
                    if step < half - 1:
                        self.send("b", step, h)
                    self.send("q", step, h)
        for copy in self.started:
            copy.wait()
        for (way, step, h), copy in self.sent.items():
            copy.wait_send()
            if way in "pq":
                copy.wait_recv()


def gather_scratch(chips):
    dma = pltpu.SemaphoreType.DMA
    return [dma((SPLIT,))] + [dma(((chips // 2 + 1) * SPLIT,))] * 8


def gather_kernel(reg, dev, own, full, *scratch):
    ring = Ring(reg, dev)
    ring.barrier()
    gather = Gather(ring, False, own, full, scratch)
    for h in range(SPLIT):
        gather.start(h)
    gather.finish()


def image_kernel(reg, dev, part, full, shard, *scratch):
    ring = Ring(reg, dev)
    ring.barrier()
    gather = Gather(ring, True, shard, full, scratch[11:])
    reduce_scatter(ring, True, part, shard, gather.start, scratch[:11])
    gather.finish()


def scatter_kernel(reg, dev, part, out, *scratch):
    ring = Ring(reg, dev)
    ring.barrier()
    reduce_scatter(ring, False, part, out, lambda h: None, scratch)


def remote_params(collective_id):
    return pltpu.CompilerParams(
        collective_id=collective_id, has_side_effects=True, vmem_limit_bytes=VMEM_LIMIT
    )


def multiply_kernel(transposed, order, keep, pos, take, blocks, table, out):
    count = blocks.shape[0]
    zero = jnp.zeros(out.shape[1:], out.dtype)

    @pl.loop(0, out.shape[0])
    def _(i):
        out[i] = zero

    contract = ((0,), (0,)) if transposed else ((1,), (0,))

    def step(i, total):
        term = lax.dot_general(
            blocks[order[i]], table[take[i]], (contract, ((), ())),
            preferred_element_type=jnp.float32,
        )
        total = jnp.where(keep[i] == 1, total, 0.0) + term
        out[pos[i]] = total.astype(out.dtype)
        return total

    lax.fori_loop(0, count, step, jnp.zeros(out.shape[1:], jnp.float32), unroll=4)


def multiply(transposed, plan, blocks, table, positions):
    count, cells, _ = blocks.shape
    rows, _, columns = table.shape
    held = (rows + positions) * cells * columns * 2
    pieces = 1 if held <= 40 * 2**20 else 2
    width = columns // pieces
    once = pl.Buffered(1)
    return pl.pallas_call(
        functools.partial(multiply_kernel, transposed),
        out_shape=jax.ShapeDtypeStruct((positions, cells, columns), jnp.bfloat16),
        grid_spec=pltpu.PrefetchScalarGridSpec(
            num_scalar_prefetch=4,
            grid=(pieces,),
            in_specs=[
                pl.BlockSpec((count, cells, cells), lambda i, *_: (0, 0, 0), pipeline_mode=once),
                pl.BlockSpec((rows, cells, width), lambda i, *_: (0, 0, i), pipeline_mode=once),
            ],
            out_specs=pl.BlockSpec((positions, cells, width), lambda i, *_: (0, 0, i), pipeline_mode=once),
        ),
        compiler_params=pltpu.CompilerParams(vmem_limit_bytes=VMEM_LIMIT),
    )(*plan, blocks, table)


class HalfGather:
    def __init__(self, ring, by_dev, full, scratch):
        self.ring, self.by_dev, self.full, self.sems = ring, by_dev, full, scratch
        self.blocks = full.shape[0] // (2 * ring.chips)
        self.size = self.blocks // PIECES
        self.sent = {}

    def send(self, way, step, h):
        ring = self.ring
        steps = ring.sign * {"a": -step, "b": step, "p": -step, "q": step}[way]
        first = ring.chunk(self.by_dev, steps) * self.blocks + h * self.size
        piece = self.full.at[pl.ds(first, self.size)]
        i = "abpq".index(way)
        index = step * PIECES + h
        copy = remote(
            piece, piece, self.sems[2 * i].at[index], self.sems[2 * i + 1].at[index],
            ring.partners()[min(i, 2)],
        )
        copy.start()
        self.sent[way, step, h] = copy

    def start(self, h):
        self.send("a", 0, h)
        if self.ring.half > 1:
            self.send("b", 0, h)
        self.send("p", 0, h)

    def step(self, step, work):
        half = self.ring.half
        for h in range(PIECES):
            work()
            self.sent["a", step - 1, h].wait_recv()
            if step < half:
                self.send("a", step, h)
            self.send("p", step, h)
            if step < half:
                work()
                self.sent["b", step - 1, h].wait_recv()
                if step < half - 1:
                    self.send("b", step, h)
                self.send("q", step, h)

    def advance(self, work, first=1, end=None):
        for step in range(first, end or self.ring.half):
            self.step(step, work)

    def tail(self):
        self.step(self.ring.half, lambda: None)
        for (way, step, h), copy in self.sent.items():
            if way in "pq":
                copy.wait_recv()

    def drain(self):
        for copy in self.sent.values():
            copy.wait_send()


class HalfScatter:
    def __init__(self, ring, by_dev, part, scratch):
        self.ring, self.by_dev, self.part = ring, by_dev, part
        self.theirs, self.from_a, self.from_b = scratch[:3]
        self.pair_send, self.pair_recv, self.a_send, self.a_recv, self.b_send, self.b_recv = scratch[3:]
        self.order = order_of_use(ring.half)
        self.blocks = part.shape[0] // (2 * ring.chips)
        self.size = self.blocks // PIECES
        self.pairs, self.sent = [], {}

    def pair(self):
        j = len(self.pairs)
        if j == len(self.order):
            return
        ring = self.ring
        steps = scatter_steps(ring.half, *self.order[j])
        first = ring.chunk(self.by_dev, -ring.sign * steps, 1) * self.blocks
        copy = remote(
            self.part.at[pl.ds(first, self.blocks)], self.theirs.at[pl.ds(j * self.blocks, self.blocks)],
            self.pair_send.at[j], self.pair_recv.at[j], ring.device(0, 1),
        )
        copy.start()
        self.pairs.append(copy)

    def chunk(self, j, work, store, after):
        ring, half = self.ring, self.ring.half
        way, step = self.order[j]
        work()
        self.pairs[j].wait_recv()
        self.pair()
        to_a, to_b, _ = ring.partners()
        for h in range(PIECES):
            first = ring.chunk(self.by_dev, ring.sign * scatter_steps(half, way, step)) * self.blocks
            mine = self.part.at[pl.ds(first + h * self.size, self.size)]
            refs = [mine, self.theirs.at[pl.ds(j * self.blocks + h * self.size, self.size)]]
            before = [("a", half - 1), ("b", half - 2)] if way == "own" else [(way, step - 1)]
            for w, s in before:
                if s >= 0:
                    work()
                    self.sent[w, s, h].wait_recv()
                    landing = self.from_a if w == "a" else self.from_b
                    refs.append(landing.at[pl.ds(s * self.blocks + h * self.size, self.size)])
            put = (lambda i, v: store(h * self.size + i, v)) if way == "own" else None

            @pl.loop(0, self.size)
            def _(i):
                total = refs[0][i].astype(jnp.float32)
                for ref in refs[1:]:
                    total += ref[i].astype(jnp.float32)
                if put is None:
                    mine[i] = total.astype(mine.dtype)
                else:
                    put(i, total)

            if way == "own":
                after(h)
                continue
            landing, send, recv, who = (
                (self.from_a, self.a_send, self.a_recv, to_a)
                if way == "a"
                else (self.from_b, self.b_send, self.b_recv, to_b)
            )
            copy = remote(
                mine, landing.at[pl.ds(step * self.blocks + h * self.size, self.size)],
                send.at[step * PIECES + h], recv.at[step * PIECES + h], who,
            )
            copy.start()
            self.sent[way, step, h] = copy

    def start(self):
        for _ in range(AHEAD):
            self.pair()
        for j in range(len(self.order)):
            if self.order[j][1] == 0 and self.order[j][0] != "own":
                self.chunk(j, lambda: None, None, None)

    def advance(self, work, first=2, end=None):
        for j in range(first, end or len(self.order) - 1):
            self.chunk(j, work, None, None)

    def final(self, store, after=lambda h: None):
        self.chunk(len(self.order) - 1, lambda: None, store, after)

    def drain(self):
        for copy in [*self.sent.values(), *self.pairs]:
            copy.wait_send()


class Job:
    def __init__(self, transposed, plan, blocks, table, running, total, part):
        self.order, self.keep, self.take, self.last = plan
        self.blocks, self.table, self.running, self.total, self.part = blocks, table, running, total, part
        self.contract = ((0,), (0,)) if transposed else ((1,), (0,))
        self.done = 0
        self.size = blocks.shape[0] // SLICES

    def slice(self):
        if self.done == SLICES:
            return
        start = self.done * self.size
        self.done += 1

        def step(i, total):
            term = lax.dot_general(
                self.blocks[self.order[start + i]], self.table[self.take[start + i]],
                (self.contract, ((), ())), preferred_element_type=jnp.float32,
            )
            total = jnp.where(self.keep[start + i] == 1, total, 0.0) + term
            self.running[start + i] = total.astype(self.running.dtype)
            return total

        self.total[...] = lax.fori_loop(0, self.size, step, self.total[...], unroll=self.size)

    def finish(self):
        while self.done < SLICES:
            self.slice()

        def place(p, unused):
            self.part[p] = self.running[self.last[p]]
            return unused

        lax.fori_loop(0, self.part.shape[0], place, 0, unroll=2)


def fused_kernel(reg, dev, *refs):
    forward_plan, backward_plan, refs = refs[:4], refs[4:8], refs[8:]
    (footprints, probe_matrix, image_out, source_out), refs = refs[:4], refs[4:]
    blocks, probe, image, part, source_part = refs[0], refs[1:3], refs[3:5], refs[5:7], refs[7:9]
    running, total, blocks_sem, probe_sem, image_sem = refs[9:14]
    refs = refs[14:]
    gathers, scatters = [refs[8 * i : 8 * i + 8] for i in range(4)], [refs[32 + 9 * i : 41 + 9 * i] for i in range(4)]
    idle = lambda: None
    ring = Ring(reg, dev)
    cells = blocks.shape[1]
    own_probe = ring.chunk(False, 0) * (probe_matrix.shape[0] // cells)
    own_image = ring.chunk(True, 0) * (image[0].shape[0] // (2 * ring.chips))
    width = probe_matrix.shape[1] // 2
    loads = []
    for h in range(2):
        for b in range(probe_matrix.shape[0] // cells):
            copy = pltpu.make_async_copy(
                probe_matrix.at[pl.ds(b * cells, cells), pl.ds(h * width, width)],
                probe[h].at[own_probe + b], probe_sem.at[h, b],
            )
            copy.start()
            loads.append(copy)
    load_blocks = pltpu.make_async_copy(footprints, blocks, blocks_sem)
    load_blocks.start()
    ring.barrier()
    for copy in loads:
        copy.wait()
    running[running.shape[0] - 1] = jnp.zeros(running.shape[1:], running.dtype)
    total[...] = jnp.zeros_like(total)

    spread = [HalfGather(ring, False, probe[h], gathers[h]) for h in range(2)]
    forward = [Job(False, forward_plan, blocks, probe[h], running, total, part[h]) for h in range(2)]
    gather = [HalfGather(ring, True, image[h], gathers[2 + h]) for h in range(2)]
    scatter = [HalfScatter(ring, True, part[h], scatters[h]) for h in range(2)]
    backward = [Job(True, backward_plan, blocks, image[h], running, total, source_part[h]) for h in range(2)]
    collect = [HalfScatter(ring, False, source_part[h], scatters[2 + h]) for h in range(2)]

    def start_all(phase):
        for h in range(PIECES):
            phase.start(h)

    def keep_image(h):
        def store(i, value):
            image[h][own_image + i] = value.astype(image[h].dtype)
        return store

    def keep_source(h):
        def store(i, value):
            source_out[pl.ds(pl.multiple_of(i * cells, cells), cells), h * width : (h + 1) * width] = value
        return store

    outs = []

    def write_image(h):
        count = image_out.shape[0] // cells
        first = lax.axis_index("dev") * count
        for b in range(count):
            copy = pltpu.make_async_copy(
                image[h].at[first + b],
                image_out.at[pl.ds(b * cells, cells), pl.ds(h * width, width)], image_sem.at[h, b],
            )
            copy.start()
            outs.append(copy)

    last = ring.half - 1
    late = len(scatter[0].order) - 3
    start_all(spread[0])
    spread[0].advance(idle, 1, last)
    start_all(spread[1])
    spread[0].advance(idle, last)
    spread[0].tail()
    load_blocks.wait()
    spread[1].advance(forward[0].slice)
    forward[0].finish()
    scatter[0].start()
    spread[1].tail()
    scatter[0].advance(forward[1].slice, 2, late)
    forward[1].finish()
    scatter[1].start()
    scatter[0].advance(idle, late)
    scatter[0].final(keep_image(0), gather[0].start)
    scatter[1].advance(idle)
    gather[0].advance(idle, 1, 2)
    scatter[1].final(keep_image(1))
    gather[0].advance(idle, 2, last)
    start_all(gather[1])
    gather[0].advance(idle, last)
    gather[0].tail()
    write_image(0)
    gather[1].advance(backward[0].slice)
    backward[0].finish()
    collect[0].start()
    gather[1].tail()
    write_image(1)
    collect[0].advance(backward[1].slice, 2, late)
    backward[1].finish()
    collect[1].start()
    collect[0].advance(idle, late)
    collect[0].final(keep_source(0))
    collect[1].advance(idle)
    collect[1].final(keep_source(1))
    for phase in (*spread, *scatter, *gather, *collect):
        phase.drain()
    for copy in outs:
        copy.wait()


def half_scatter_scratch(chips, blocks, cells, width):
    half = chips // 2
    dma = pltpu.SemaphoreType.DMA
    buffer = lambda n: pltpu.VMEM((n * blocks, cells, width), jnp.bfloat16)
    return [buffer(chips), buffer(half), buffer(max(half - 1, 1)), dma((chips,)), dma((chips,))] + [
        dma((half * PIECES,))
    ] * 4


def fused(reg, dev, forward_plan, backward_plan, footprints, probe_matrix, receptors):
    count, cells, _ = footprints.shape
    chips, devices = reg // 2 * dev, reg * dev
    width = probe_matrix.shape[1] // 2
    own_sources, own_receptors = probe_matrix.shape[0] // cells, receptors // devices
    sources = own_sources * devices
    buffer = lambda n: pltpu.VMEM((n, cells, width), jnp.bfloat16)
    dma = pltpu.SemaphoreType.DMA
    scratch = (
        [pltpu.VMEM(footprints.shape, jnp.bfloat16)]
        + [buffer(sources)] * 2 + [buffer(receptors)] * 4 + [buffer(sources)] * 2
        + [buffer(count + 1), pltpu.VMEM((cells, width), jnp.float32)]
        + [dma(()), dma((2, own_sources)), dma((2, own_receptors * reg))]
        + [dma(((chips // 2 + 1) * PIECES,))] * 32
        + half_scatter_scratch(chips, own_receptors, cells, width) * 2
        + half_scatter_scratch(chips, own_sources, cells, width) * 2
    )
    return pl.pallas_call(
        functools.partial(fused_kernel, reg, dev),
        out_shape=(
            jax.ShapeDtypeStruct((receptors // dev * cells, 2 * width), jnp.bfloat16),
            jax.ShapeDtypeStruct(probe_matrix.shape, jnp.float32),
        ),
        in_specs=[pl.BlockSpec(memory_space=pltpu.SMEM)] * 8 + [ANY] * 2,
        out_specs=(ANY, pl.BlockSpec(memory_space=pltpu.VMEM)),
        scratch_shapes=scratch,
        compiler_params=remote_params(4),
    )(*forward_plan, *backward_plan, footprints, probe_matrix)


def with_last(plan, positions):
    order, keep, pos, take = plan
    hit = pos[None, :] == jnp.arange(positions, dtype=jnp.int32)[:, None]
    place = jnp.max(jnp.where(hit, jnp.arange(pos.shape[0], dtype=jnp.int32)[None, :], -1), axis=1)
    return order, keep, take, jnp.where(place < 0, pos.shape[0], place)


def look_up(place, index):
    hit = index[:, None] == jnp.arange(place.shape[0], dtype=jnp.int32)[None, :]
    return jnp.sum(jnp.where(hit, place[None, :], 0), axis=1)


def sorted_plan(pos, take):
    count = pos.shape[0]
    number = jnp.arange(count, dtype=jnp.int32)
    key = pos * count + number
    rank = jnp.sum((key[None, :] < key[:, None]).astype(jnp.int32), axis=1)
    hit = rank[None, :] == number[:, None]
    pick = lambda values: jnp.sum(jnp.where(hit, values[None, :], 0), axis=1)
    pos_sorted = pick(pos)
    before = jnp.concatenate([jnp.full((1,), -1, jnp.int32), pos_sorted[:-1]])
    return pick(number), (pos_sorted == before).astype(jnp.int32), pos_sorted, pick(take)


def local(footprints, block_coords, receptor_place, source_place, probe_matrix):
    cells = footprints.shape[1]
    columns = probe_matrix.shape[1]
    reg, dev = lax.axis_size("reg"), lax.axis_size("dev")
    chips, devices = reg // 2 * dev, reg * dev
    receptors = receptor_place.shape[0]
    sources = probe_matrix.shape[0] * devices // cells
    bf16 = jnp.bfloat16

    pos_rec = look_up(receptor_place, block_coords[:, 0])
    pos_src = look_up(source_place, block_coords[:, 1])
    forward_plan = sorted_plan(pos_rec, pos_src)
    backward_plan = sorted_plan(pos_src, pos_rec)

    block_bytes = 2 * cells * columns // 2
    blocks_held = 2 * (3 * receptors + 3 * sources) + 2 * footprints.shape[0]
    per_device = [receptors // devices, sources // devices]
    divides = all(n % PIECES == 0 for n in per_device)
    divides = divides and columns % 256 == 0 and footprints.shape[0] % SLICES == 0
    if blocks_held * block_bytes <= 48 * 2**20 and divides and chips >= 8:
        return fused(
            reg, dev, with_last(forward_plan, receptors), with_last(backward_plan, sources),
            footprints, probe_matrix, receptors,
        )

    probe_rows = probe_matrix.shape[0]
    probe = pl.pallas_call(
        functools.partial(gather_kernel, reg, dev),
        out_shape=jax.ShapeDtypeStruct((devices, probe_rows, columns), bf16),
        in_specs=[ANY], out_specs=ANY,
        scratch_shapes=gather_scratch(chips),
        compiler_params=remote_params(1),
    )(probe_matrix)

    receptor_part = multiply(False, forward_plan, footprints, probe.reshape(sources, cells, columns), receptors)

    image_rows = receptors * cells // devices
    image = pl.pallas_call(
        functools.partial(image_kernel, reg, dev),
        out_shape=jax.ShapeDtypeStruct((devices, image_rows, columns), bf16),
        in_specs=[ANY], out_specs=ANY,
        scratch_shapes=[pltpu.VMEM((image_rows, columns), bf16)]
        + scatter_scratch(chips, image_rows, columns) + gather_scratch(chips),
        compiler_params=remote_params(2),
    )(receptor_part.reshape(devices, image_rows, columns))
    receptor_image = lax.dynamic_slice_in_dim(image, lax.axis_index("dev") * reg, reg, 0)

    source_part = multiply(True, backward_plan, footprints, image.reshape(receptors, cells, columns), sources)

    source_image = pl.pallas_call(
        functools.partial(scatter_kernel, reg, dev),
        out_shape=jax.ShapeDtypeStruct((probe_rows, columns), jnp.float32),
        in_specs=[ANY], out_specs=pl.BlockSpec(memory_space=pltpu.VMEM),
        scratch_shapes=scatter_scratch(chips, probe_rows, columns),
        compiler_params=remote_params(3),
    )(source_part.reshape(devices, probe_rows, columns))
    return receptor_image.reshape(reg * image_rows, columns), source_image


def solution(mesh):
    return jax.shard_map(
        local,
        mesh=mesh,
        in_specs=(
            P(("grp", "reg", "dev"), None, None),
            P(("grp", "reg", "dev"), None),
            P("grp"),
            P("grp"),
            P(("grp", "reg", "dev"), None),
        ),
        out_specs=(P(("grp", "dev"), None), P(("grp", "reg", "dev"), None)),
        check_vma=False,
    )
```
